1024 devices in a mesh: replica: 16 (over x_hi, y), fsdp: 16 (over z), tensor: 4 (over x_lo, core).
Axes of the slice: x: 4 (x_hi: 2, x_lo: 2; x = x_hi * 2 + x_lo), y: 8, z: 16, core: 2. Of those that a mesh axis runs over, the one named last changes fastest.
Arguments:
- acts: bfloat16 [16, 4096, 8192], P('replica', 'fsdp', 'tensor'), may hold values from -6 to 6
- key_weight: bfloat16 [16, 512, 8192], P('replica', 'fsdp', 'tensor'), may hold values from -0.0625 to 0.0625
- key_cotangent: bfloat16 [16, 4096, 512], P('replica', 'fsdp', 'tensor'), may hold values from -1.1953125 to 1.1953125
- first_moment: float32 [16, 512, 8192], P('replica', 'fsdp', 'tensor'), may hold values from -3 to 3
- second_moment: float32 [16, 512, 8192], P('replica', 'fsdp', 'tensor'), may hold values from 0.01 to 1
- local_params: bfloat16 [16, 131072, 128], P('replica', ('fsdp', 'tensor')), may hold values from -6 to 6
- outer_params: float32 [16384, 128], P(('fsdp', 'tensor')), may hold values from -6 to 6
- outer_momentum: float32 [16384, 128], P(('fsdp', 'tensor')), may hold values from -3 to 3
- fragment_index: int32 [1], replicated, may hold values from 0 to 7
- slice_offsets: int32 [8], replicated, may hold values from 0 to 1792, as said below
Outputs:
- keys: bfloat16 [16, 4096, 512], P('replica', 'fsdp', 'tensor')
- new_weight: bfloat16 [16, 512, 8192], P('replica', 'fsdp', 'tensor')
- new_first: float32 [16, 512, 8192], P('replica', 'fsdp', 'tensor')
- new_second: float32 [16, 512, 8192], P('replica', 'fsdp', 'tensor')
- synced_params: float32 [16384, 128], P(('fsdp', 'tensor'))
- synced_momentum: float32 [16384, 128], P(('fsdp', 'tensor'))
The draws below stay inside these ranges and needn't reach their ends.
Inputs may be any that keep to these rules, and one draw needn't show every extreme that they name: `slice_offsets`: distinct multiples of 256, one for each fragment.
All inputs are finite; a program needn't handle non-finite values.
Results may differ from the reference program's by a relative error of at most 0.001.
Values may be sent and summed in bfloat16 or wider, within the bound.
A program may use at most 32 MiB of HBM per device.

```python
import math
import jax
import jax.numpy as jnp
from jax import lax

D = 8192
KW = 512
TOKENS = 4096
WORKERS = 16
FRAGS = 8
SLICE_ROWS = 256
LANES = 128
BLOCKS = 64
BUF_ROWS = 2048


def draw_slice_offsets(key, part):
    key = jax.random.fold_in(key, 7)
    ordering = jax.random.permutation(key, FRAGS)
    return (ordering * SLICE_ROWS).astype(jnp.int32)


def spiked(result, key, source, target, parts, factor):
    def block_of(position):
        return (jnp.arange(result.shape[position]) // (result.shape[position] // parts)).reshape((-1,) + (1,) * (result.ndim - 1 - position))

    first = jax.random.permutation(key, parts)[block_of(target)]
    other_side = (block_of(target) + parts // 2) % parts
    return jnp.where((block_of(source) == first) | (block_of(source) == other_side), factor * result, result)


def steps_of(own_key, dims, split, low, top_value):
    loudness, own = 1.0, jax.random.fold_in(own_key, 6)
    for axis_at, blocks in split:
        draws = jnp.exp(jax.random.uniform(jax.random.fold_in(own, axis_at), (blocks,), jnp.float32, low / len(split), top_value / len(split)))
        loudness = loudness * jnp.repeat(draws, dims[axis_at] // blocks).reshape([-1 if axis == axis_at else 1 for axis in range(len(dims))])
    return loudness


def centred(own_key, shape, width, reach, split=(), dtype=jnp.bfloat16):
    result = width * jax.random.normal(own_key, shape, jnp.float32)
    if split:
        result = result * steps_of(own_key, shape, split, -0.22, 0.18)
    return jnp.clip(result, -reach, reach).astype(dtype)


def bell_draw_with(rng, extent, deviation, most, shards, heavy, kind=jnp.bfloat16):
    drawn = deviation * jax.random.normal(rng, extent, jnp.float32)
    if shards:
        drawn = drawn * steps_of(rng, extent, shards, -0.22, 0.18)
    return jnp.clip(spiked(drawn, jax.random.fold_in(rng, 3), *heavy), -most, most).astype(kind)


def setup_inputs(seed: int = 0) -> dict:
    key_list = jax.random.split(jax.random.key(seed), 11)
    acts = centred(key_list[0], (WORKERS, TOKENS, D), 1.0, 6.0, ((0, 16), (1, 16), (2, 4)))
    key_weight = centred(key_list[1], (WORKERS, KW, D), D ** -0.5, 0.0625, ((0, 16), (1, 16), (2, 4)))
    key_cotangent = bell_draw_with(key_list[2], (WORKERS, TOKENS, KW), 0.2, 1.1953125, ((0, 16), (1, 16), (2, 4)), (1, 2, 16, 2.0))
    first_moment = centred(key_list[3], (WORKERS, KW, D), 0.5, 3.0, ((0, 16), (1, 16), (2, 4)), jnp.float32)
    second_moment = jnp.clip(jnp.exp(math.log(1.0) - 4.6051702 * jax.random.uniform(key_list[4], (WORKERS, KW, D), jnp.float32) ** steps_of(key_list[4], (WORKERS, KW, D), ((0, 16), (1, 16), (2, 4)), -0.2, 0.2)), 0.01, 1.0)
    local_params = centred(key_list[5], (WORKERS, BLOCKS * BUF_ROWS, LANES), 1.0, 6.0, ((0, 16), (1, 64)))
    outer_params = centred(key_list[6], (BLOCKS * SLICE_ROWS, LANES), 1.0, 6.0, ((0, 64),), jnp.float32)
    outer_momentum = centred(key_list[7], (BLOCKS * SLICE_ROWS, LANES), 0.5, 3.0, ((0, 64),), jnp.float32)
    fragment_index = jax.random.randint(key_list[8], (1,), 0, FRAGS).astype(jnp.int32)
    slice_offsets = draw_slice_offsets(jax.random.fold_in(key_list[10], 71), 0)
    return {"acts": acts, "key_weight": key_weight, "key_cotangent": key_cotangent, "first_moment": first_moment, "second_moment": second_moment, "local_params": local_params, "outer_params": outer_params, "outer_momentum": outer_momentum, "fragment_index": fragment_index, "slice_offsets": slice_offsets}


beta_first = 0.9
beta_second = 0.95
adam_rate = 0.001
adam_eps = 1e-08
decay_coef = 0.1
outer_rate = 0.7
momentum_coef = 0.9

def inner_worker(operands):
    tokens_here, weight_here, cotangent, first_here, second_here = operands
    keys_here = jnp.dot(tokens_here, weight_here.T, preferred_element_type=jnp.float32).astype(jnp.bfloat16)
    gradient = lax.dot_general(cotangent, tokens_here, (((0,), (0,)), ((), ())), preferred_element_type=jnp.float32)
    first_next = beta_first * first_here + (1.0 - beta_first) * gradient
    second_next = beta_second * second_here + (1.0 - beta_second) * gradient * gradient
    weight_float = weight_here.astype(jnp.float32)
    weight_next = weight_float - adam_rate * (first_next / (jnp.sqrt(second_next) + adam_eps) + decay_coef * weight_float)
    return (keys_here, weight_next.astype(jnp.bfloat16), first_next, second_next)

def reference(acts, key_weight, key_cotangent, first_moment, second_moment, local_params, outer_params, outer_momentum, fragment_index, slice_offsets):
    keys, new_weight, new_first, new_second = lax.map(inner_worker, (acts, key_weight, key_cotangent, first_moment, second_moment))
    offset = slice_offsets[fragment_index[0]].astype(jnp.int32)
    blocked = local_params.reshape(WORKERS, BLOCKS, BUF_ROWS, LANES)
    picked = lax.dynamic_slice_in_dim(blocked, offset, SLICE_ROWS, 2)
    local_slice = picked.reshape(WORKERS, BLOCKS * SLICE_ROWS, LANES).astype(jnp.float32)
    mean_delta = lax.optimization_barrier(jnp.sum(outer_params[None] - local_slice, axis=0)) / WORKERS
    synced_momentum = momentum_coef * outer_momentum + mean_delta
    synced_params = outer_params - outer_rate * (mean_delta + momentum_coef * synced_momentum)
    return (keys, new_weight, new_first, new_second, synced_params, synced_momentum)
```

```python
import functools

import jax
import jax.numpy as jnp
from jax import lax
from jax.experimental import pallas as pl
from jax.experimental.pallas import tpu as pltpu
from jax.sharding import PartitionSpec as P

MESH = pl.DeviceIdType.MESH
F32 = jnp.float32
LAG = 5
TOP = 32700.0
STEPS = 4.0

beta_first = 0.9
beta_second = 0.95
adam_rate = 0.001
adam_eps = 1e-08
decay_coef = 0.1
outer_rate = 0.7
momentum_coef = 0.9


def kernel(
    n, T, R,
    acts_h, w_h, cot_h, m1_h, m2_h, loc_h, outer_h, mom_h, frag_s, offs_s,
    keys_o, nw_o, nf_o, ns_o, sp_o, sm_o,
    acts_v, w_v, cot_v, g_v, m1_v, m2_v, nw_v, kp_v, kr_v, k_v,
    loc_v, ls_v, outer_v, mom_v, ob_v, mean_v, sp_v,
    su_v, sd_v, ru_v, rd_v,
    lsem, osem, ags, agr, rss, rsr, cs, cr, ks, kr, oas, oar, obs, obr,
):
    z = lax.axis_index("fsdp")
    t = lax.axis_index("tensor")
    r = lax.axis_index("replica")
    h = n // 2
    up = lax.rem(z + 1, n)
    down = lax.rem(z + n - 1, n)
    rows = w_h.shape[1]
    half = rows // 2
    width = w_h.shape[2]
    lanes = min(128, width)
    tiles = width // lanes
    kt = kp_v.shape[2]
    per = n // T
    orow = outer_h.shape[0] // R
    msgs = 2 * h - 1

    def at(axis, index):
        return dict(device_id={axis: index}, device_id_type=MESH)

    core = lax.rem(t, 2)
    side = t // 2
    sib = t + 1 - 2 * core
    peers = [sib, lax.rem(t + 2, 4), lax.rem(sib + 2, 4)]

    def load(src, dst, i):
        c = pltpu.make_async_copy(src, dst, lsem.at[i])
        c.start()
        return c

    l_cot = load(cot_h.at[0], cot_v.at[t], 0)
    l_acts = load(acts_h.at[0], acts_v, 1)
    l_loc = load(loc_h.at[0], loc_v, 2)
    l_outer = load(outer_h, outer_v, 3)
    l_w = load(w_h.at[0], w_v.at[z], 4)
    l_mom = load(mom_h, mom_v, 5)
    l_m1 = load(m1_h.at[0], m1_v, 6)
    l_m2 = load(m2_h.at[0], m2_v, 7)

    barrier = pltpu.get_barrier_semaphore()
    for index in (up, down):
        pl.semaphore_signal(barrier, inc=1, **at("fsdp", index))
    for p in peers:
        pl.semaphore_signal(barrier, inc=1, **at("tensor", p))
    for i in range(1, R):
        pl.semaphore_signal(barrier, inc=1, **at("replica", lax.rem(r + i, R)))
    pl.semaphore_wait(barrier, 2 + len(peers) + R - 1)

    def ag(m, way, receiving=False):
        j, sub = m // 2, (m % 2 if way == 0 else 1 - m % 2)
        j = j + (1 if receiving else 0)
        owner = lax.rem(z + n - j, n) if way == 0 else lax.rem(z + j, n)
        cut = pl.ds(sub * half, half)
        src = w_h.at[0, cut] if (m // 2 == 0 and not receiving) else w_v.at[owner, cut]
        return pltpu.make_async_remote_copy(
            src_ref=src,
            dst_ref=w_v.at[owner, cut],
            send_sem=ags.at[way, m],
            recv_sem=agr.at[way, m],
            **at("fsdp", up if way == 0 else down),
        )

    sends = []

    def ag_tick(m):
        for way in (0, 1):
            if m >= 2:
                ag(m - 2, way, True).wait_recv()
            c = ag(m, way)
            c.start()
            sends.append(c)

    def rs_msg(i, way):
        main = 0 if way == 0 else 1
        if i % 2 == 0:
            return i // 2, main
        return (i + 1) // 2, 1 - main

    def rs(i, way):
        s_buf, r_buf = (su_v, ru_v) if way == 0 else (sd_v, rd_v)
        return pltpu.make_async_remote_copy(
            src_ref=s_buf.at[i],
            dst_ref=r_buf.at[i],
            send_sem=rss.at[way, i],
            recv_sem=rsr.at[way, i],
            **at("fsdp", up if way == 0 else down),
        )

    def scale_of(buf, i):
        code = buf[i, :, width:width + lanes].astype(jnp.int32).astype(F32)
        return jnp.exp2(code * (1.0 / STEPS)) * (1.0 / TOP)

    def rs_tick(i):
        for way in (0, 1):
            s, sub = rs_msg(i, way)
            s_buf, r_buf = (su_v, ru_v) if way == 0 else (sd_v, rd_v)
            d = lax.rem(z + n + h - s, n) if way == 0 else lax.rem(z + n - h + s, n)
            got = i >= 2
            if got:
                rs(i - 2, way).wait_recv()
                scale = scale_of(r_buf, i - 2)
            sums, most = [], None
            for c in range(tiles):
                cols = slice(c * lanes, (c + 1) * lanes)
                x = g_v[d, sub * half:(sub + 1) * half, cols]
                if got:
                    x = x + r_buf[i - 2, :, cols].astype(jnp.int32).astype(F32) * scale
                sums.append(x)
                a = jnp.abs(x)
                most = a if most is None else jnp.maximum(most, a)
            most = jnp.max(most, axis=0, keepdims=True)
            code = jnp.ceil(STEPS * jnp.log2(jnp.maximum(most, 1e-30)))
            inv = TOP * jnp.exp2(code * (-1.0 / STEPS))
            for c in range(tiles):
                cols = slice(c * lanes, (c + 1) * lanes)
                s_buf[i, :, cols] = jnp.round(sums[c] * inv).astype(jnp.int32).astype(jnp.int16)
            s_buf[i, :, width:width + lanes] = jnp.broadcast_to(
                code.astype(jnp.int32), (half, lanes)
            ).astype(jnp.int16)
            c = rs(i, way)
            c.start()
            sends.append(c)

    def cot_copy(k, receiving=False):
        slot = peers[k] if receiving else t
        return pltpu.make_async_remote_copy(
            src_ref=cot_v.at[slot] if receiving else cot_h.at[0],
            dst_ref=cot_v.at[slot],
            send_sem=cs.at[k],
            recv_sem=cr.at[k],
            **at("tensor", peers[k]),
        )

    def key_copy(k):
        return pltpu.make_async_remote_copy(
            src_ref=kp_v.at[peers[k]],
            dst_ref=kr_v.at[k],
            send_sem=ks.at[k],
            recv_sem=kr.at[k],
            **at("tensor", peers[k]),
        )

    def start_cot():
        for k in (1, 2, 0):
            c = cot_copy(k)
            c.start()
            sends.append(c)

    def slice_copy(i, receiving=False):
        to = lax.rem(r + i, R)
        slot = lax.rem(r + R - i, R) if receiving else r
        return pltpu.make_async_remote_copy(
            src_ref=ls_v.at[pl.ds(pl.multiple_of(to * orow, orow), orow)],
            dst_ref=ob_v.at[slot],
            send_sem=oas.at[i],
            recv_sem=oar.at[i],
            **at("replica", to),
        )

    def mean_copy(i, receiving=False):
        to = lax.rem(r + i, R)
        slot = lax.rem(r + R - i, R) if receiving else r
        cut = pl.ds(pl.multiple_of(slot * orow, orow), orow)
        return pltpu.make_async_remote_copy(
            src_ref=mean_v.at[cut],
            dst_ref=mean_v.at[cut],
            send_sem=obs.at[i],
            recv_sem=obr.at[i],
            **at("replica", to),
        )

    def outer_send():
        l_loc.wait()
        size = ls_v.shape[0]
        offset = offs_s[0]
        for f in range(1, offs_s.shape[0]):
            offset = jnp.where(frag_s[0] == f, offs_s[f], offset)
        picked = loc_v[:size, :].astype(F32)
        for b in range(1, loc_v.shape[0] // size):
            piece = loc_v[b * size:(b + 1) * size, :].astype(F32)
            picked = jnp.where(offset == b * size, piece, picked)
        ls_v[...] = picked.astype(jnp.bfloat16)
        for i in range(1, R):
            c = slice_copy(i)
            c.start()
            sends.append(c)

    def outer_mean():
        l_outer.wait()
        mine = pl.ds(pl.multiple_of(r * orow, orow), orow)
        base = outer_v[mine]
        total = base - ls_v[mine].astype(F32)
        for i in range(1, R):
            slice_copy(i, True).wait_recv()
            total = total + (base - ob_v[lax.rem(r + R - i, R)].astype(F32))
        mean_v[mine] = total / R
        for i in range(1, R):
            c = mean_copy(i)
            c.start()
            sends.append(c)

    outs = []

    def store(src, dst, i):
        c = pltpu.make_async_copy(src, dst, osem.at[i])
        c.start()
        outs.append(c)

    def outer_step():
        l_mom.wait()
        for i in range(1, R):
            mean_copy(i, True).wait_recv()
        mean = mean_v[...]
        moment = momentum_coef * mom_v[...] + mean
        mom_v[...] = moment
        sp_v[...] = outer_v[...] - outer_rate * (mean + momentum_coef * moment)
        store(mom_v, sm_o, 0)
        store(sp_v, sp_o, 1)

    def gradient():
        l_acts.wait()
        l_cot.wait()
        for k in range(len(peers)):
            cot_copy(k, True).wait_recv()
        cot = jnp.concatenate([cot_v[k] for k in range(T)], axis=1)
        piece = width // 4
        for c in range(4):
            cols = slice(c * piece, (c + 1) * piece)
            g_v[:, :, cols] = lax.dot_general(
                cot, acts_v[:, cols], (((0,), (0,)), ((), ())), preferred_element_type=F32
            ).reshape(n, rows, piece)

    def keys_part(far):
        u = (1 - side) if far else side
        block = w_v[pl.ds(u * 2 * per, 2 * per)].reshape(2 * per * rows, width)
        got = lax.dot_general(
            acts_v[...], block, (((1,), (1,)), ((), ())), preferred_element_type=F32
        )
        kp_v[2 * u] = got[:, :kt]
        kp_v[2 * u + 1] = got[:, kt:]
        for k in ((1, 2) if far else (0,)):
            c = key_copy(k)
            c.start()
            sends.append(c)

    def keys_end():
        for k in range(len(peers)):
            key_copy(k).wait_recv()
        k_v[...] = (((kp_v[t] + kr_v[0]) + kr_v[1]) + kr_v[2]).astype(jnp.bfloat16)
        store(k_v, keys_o.at[0], 2)

    last = msgs + LAG
    for tick in range(last):
        if tick < msgs:
            ag_tick(tick)
        if tick >= LAG:
            rs_tick(tick - LAG)
        if tick == 1:
            start_cot()
        if tick == min(2, msgs - 1):
            outer_send()
        if tick == LAG - 1:
            gradient()
        if tick == LAG + 1:
            outer_mean()
        if tick == msgs - 1:
            l_w.wait()
            for m in (msgs - 2, msgs - 1):
                for way in (0, 1):
                    ag(m, way, True).wait_recv()
            keys_part(True)
        if tick == msgs:
            keys_part(False)
            outer_step()
    keys_end()

    l_m1.wait()
    l_m2.wait()

    def finish(sub):
        iu = msgs - 1 if sub == 0 else msgs - 2
        idn = msgs - 2 if sub == 0 else msgs - 1
        rs(iu, 0).wait_recv()
        rs(idn, 1).wait_recv()
        su, sd = scale_of(ru_v, iu), scale_of(rd_v, idn)
        rr = slice(sub * half, (sub + 1) * half)
        for c in range(tiles):
            cols = slice(c * lanes, (c + 1) * lanes)
            grad = (
                g_v[z, rr, cols]
                + ru_v[iu, :, cols].astype(jnp.int32).astype(F32) * su
                + rd_v[idn, :, cols].astype(jnp.int32).astype(F32) * sd
            )
            first = beta_first * m1_v[rr, cols] + (1.0 - beta_first) * grad
            second = beta_second * m2_v[rr, cols] + (1.0 - beta_second) * grad * grad
            w = w_v[z, rr, cols].astype(F32)
            new = w - adam_rate * (first / (jnp.sqrt(second) + adam_eps) + decay_coef * w)
            nw_v[rr, cols] = new.astype(jnp.bfloat16)
            m1_v[rr, cols] = first
            m2_v[rr, cols] = second
        cut = pl.ds(sub * half, half)
        store(m1_v.at[cut], nf_o.at[0, cut], 3 + 3 * sub)
        store(m2_v.at[cut], ns_o.at[0, cut], 4 + 3 * sub)
        store(nw_v.at[cut], nw_o.at[0, cut], 5 + 3 * sub)

    finish(0)
    finish(1)
    for c in sends:
        c.wait_send()
    for c in outs:
        c.wait()


def solution(mesh):
    n, T, R = mesh.shape["fsdp"], mesh.shape["tensor"], mesh.shape["replica"]

    def on_device(acts, w, cot, m1, m2, loc, outer, mom, frag, offs):
        tok, width = acts.shape[1:]
        rows = w.shape[1]
        half = rows // 2
        kt = cot.shape[2]
        msgs = n - 1
        lanes = min(128, width)
        bf16 = jnp.bfloat16
        orow = outer.shape[0] // R
        any_ = pl.BlockSpec(memory_space=pl.ANY)
        smem = pl.BlockSpec(memory_space=pltpu.SMEM)
        ring = pltpu.VMEM((msgs, half, width + lanes), jnp.int16)
        dma = pltpu.SemaphoreType.DMA
        return pl.pallas_call(
            functools.partial(kernel, n, T, R),
            out_shape=(
                jax.ShapeDtypeStruct((1, tok, kt), bf16),
                jax.ShapeDtypeStruct(w.shape, bf16),
                jax.ShapeDtypeStruct(m1.shape, F32),
                jax.ShapeDtypeStruct(m2.shape, F32),
                jax.ShapeDtypeStruct(outer.shape, F32),
                jax.ShapeDtypeStruct(mom.shape, F32),
            ),
            in_specs=[pl.BlockSpec(memory_space=pltpu.HBM)] * 8 + [smem] * 2,
            out_specs=[any_] * 6,
            scratch_shapes=[
                pltpu.VMEM((tok, width), bf16),
                pltpu.VMEM((n, rows, width), bf16),
                pltpu.VMEM((T, tok, kt), bf16),
                pltpu.VMEM((n, rows, width), F32),
                pltpu.VMEM((rows, width), F32),
                pltpu.VMEM((rows, width), F32),
                pltpu.VMEM((rows, width), bf16),
                pltpu.VMEM((T, tok, kt), F32),
                pltpu.VMEM((T - 1, tok, kt), F32),
                pltpu.VMEM((tok, kt), bf16),
                pltpu.VMEM(loc.shape[1:], bf16),
                pltpu.VMEM(outer.shape, bf16),
                pltpu.VMEM(outer.shape, F32),
                pltpu.VMEM(outer.shape, F32),
                pltpu.VMEM((R, orow, outer.shape[1]), bf16),
                pltpu.VMEM(outer.shape, F32),
                pltpu.VMEM(outer.shape, F32),
                ring, ring, ring, ring,
                dma((8,)),
                dma((9,)),
                dma((2, msgs)),
                dma((2, msgs)),
                dma((2, msgs)),
                dma((2, msgs)),
                dma((T - 1,)),
                dma((T - 1,)),
                dma((T - 1,)),
                dma((T - 1,)),
                dma((R,)),
                dma((R,)),
                dma((R,)),
                dma((R,)),
            ],
            compiler_params=pltpu.CompilerParams(
                collective_id=0, has_side_effects=True, vmem_limit_bytes=60 * 2**20
            ),
        )(acts, w, cot, m1, m2, loc, outer, mom, frag, offs)

    big = P("replica", "fsdp", "tensor")
    flat = P(("fsdp", "tensor"), None)
    return jax.shard_map(
        on_device,
        mesh=mesh,
        in_specs=(big, big, big, big, big, P("replica", ("fsdp", "tensor"), None), flat, flat, P(), P()),
        out_specs=(big, big, big, big, flat, flat),
        check_vma=False,
    )
```

```python
import functools

import jax
import jax.numpy as jnp
from jax import lax
from jax.experimental import pallas as pl
from jax.experimental.pallas import tpu as pltpu
from jax.sharding import PartitionSpec as P

MESH = pl.DeviceIdType.MESH
F32 = jnp.float32
LAG = 3
CA = 1
CR = 1
TOP = 32700.0
STEPS = 4.0

beta_first = 0.9
beta_second = 0.95
adam_rate = 0.001
adam_eps = 1e-08
decay_coef = 0.1
outer_rate = 0.7
momentum_coef = 0.9


def kernel(
    n, T, R,
    acts_h, w_h, cot_h, m1_h, m2_h, loc_h, outer_h, mom_h, frag_s, offs_s,
    keys_o, nw_o, nf_o, ns_o, sp_o, sm_o,
    acts_v, w_v, cot_v, g_v, m1_v, m2_v, nw_v, kp_v, kr_v, k_v,
    loc_v, ls_v, outer_v, mom_v, ob_v, mean_v, sp_v,
    su_v, sd_v, ru_v, rd_v,
    lsem, osem, ags, agr, rss, rsr, cs, cr, ks, kr, oas, oar, obs, obr,
):
    z = lax.axis_index("fsdp")
    t = lax.axis_index("tensor")
    r = lax.axis_index("replica")
    h = n // 2
    up = lax.rem(z + 1, n)
    down = lax.rem(z + n - 1, n)
    rows = w_h.shape[1]
    half = rows // 2
    width = w_h.shape[2]
    lanes = min(128, width)
    kt = kp_v.shape[2]
    per = n // T
    orow = outer_h.shape[0] // R
    msgs = 2 * h - 1

    def at(axis, index):
        return dict(device_id={axis: index}, device_id_type=MESH)

    core = lax.rem(t, 2)
    side = t // 2
    sib = t + 1 - 2 * core
    peers = [sib, lax.rem(t + 2, 4), lax.rem(sib + 2, 4)]

    def load(src, dst, i):
        c = pltpu.make_async_copy(src, dst, lsem.at[i])
        c.start()
        return c

    l_cot = load(cot_h.at[0], cot_v.at[t], 0)
    l_acts = load(acts_h.at[0], acts_v, 1)
    l_loc = load(loc_h.at[0], loc_v, 2)
    l_outer = load(outer_h, outer_v, 3)
    l_w = load(w_h.at[0], w_v.at[z], 4)
    l_mom = load(mom_h, mom_v, 5)
    l_m1 = load(m1_h.at[0], m1_v, 6)
    l_m2 = load(m2_h.at[0], m2_v, 7)

    barrier = pltpu.get_barrier_semaphore()
    for index in (up, down):
        pl.semaphore_signal(barrier, inc=1, **at("fsdp", index))
    for p in peers:
        pl.semaphore_signal(barrier, inc=1, **at("tensor", p))
    for i in range(1, R):
        pl.semaphore_signal(barrier, inc=1, **at("replica", lax.rem(r + i, R)))
    pl.semaphore_wait(barrier, 2 + len(peers) + R - 1)

    acut = width // CA

    def ag(m, way, receiving=False):
        j, q = m // (2 * CA), m % (2 * CA)
        sub, col = (q // CA if way == 0 else 1 - q // CA), q % CA
        hop = j + (1 if receiving else 0)
        owner = lax.rem(z + n - hop, n) if way == 0 else lax.rem(z + hop, n)
        cut, cols = pl.ds(sub * half, half), pl.ds(col * acut, acut)
        own = j == 0 and not receiving
        src = w_h.at[0, cut, cols] if own else w_v.at[owner, cut, cols]
        return pltpu.make_async_remote_copy(
            src_ref=src,
            dst_ref=w_v.at[owner, cut, cols],
            send_sem=ags.at[way, m],
            recv_sem=agr.at[way, m],
            **at("fsdp", up if way == 0 else down),
        )

    sends = []

    def ag_tick(m):
        for way in (0, 1):
            if m >= 2 * CA:
                ag(m - 2 * CA, way, True).wait_recv()
            c = ag(m, way)
            c.start()
            sends.append(c)

    rcut = width // CR
    rtiles = rcut // lanes

    def rs_msg(i, way):
        main = 0 if way == 0 else 1
        if i < CR:
            return 0, main, i
        k = i - CR
        q = k % (2 * CR)
        return 1 + k // (2 * CR), (1 - main if q < CR else main), q % CR

    def rs(i, way):
        s_buf, r_buf = (su_v, ru_v) if way == 0 else (sd_v, rd_v)
        return pltpu.make_async_remote_copy(
            src_ref=s_buf.at[i],
            dst_ref=r_buf.at[i],
            send_sem=rss.at[way, i],
            recv_sem=rsr.at[way, i],
            **at("fsdp", up if way == 0 else down),
        )

    def scale_of(buf, i):
        code = buf[i, :, rcut:rcut + lanes].astype(jnp.int32).astype(F32)
        return jnp.exp2(code * (1.0 / STEPS)) * (1.0 / TOP)

    def rs_tick(i):
        for way in (0, 1):
            s, sub, col = rs_msg(i, way)
            s_buf, r_buf = (su_v, ru_v) if way == 0 else (sd_v, rd_v)
            d = lax.rem(z + n + h - s, n) if way == 0 else lax.rem(z + n - h + s, n)
            last = i - 2 * CR
            if last >= 0:
                rs(last, way).wait_recv()
                scale = scale_of(r_buf, last)
            sums, most = [], None
            for c in range(rtiles):
                here = slice(c * lanes, (c + 1) * lanes)
                whole = slice(col * rcut + c * lanes, col * rcut + (c + 1) * lanes)
                x = g_v[d, sub * half:(sub + 1) * half, whole]
                if last >= 0:
                    x = x + r_buf[last, :, here].astype(jnp.int32).astype(F32) * scale
                sums.append(x)
                a = jnp.abs(x)
                most = a if most is None else jnp.maximum(most, a)
            most = jnp.max(most, axis=0, keepdims=True)
            code = jnp.ceil(STEPS * jnp.log2(jnp.maximum(most, 1e-30)))
            inv = TOP * jnp.exp2(code * (-1.0 / STEPS))
            for c in range(rtiles):
                here = slice(c * lanes, (c + 1) * lanes)
                s_buf[i, :, here] = jnp.round(sums[c] * inv).astype(jnp.int32).astype(jnp.int16)
            s_buf[i, :, rcut:rcut + lanes] = jnp.broadcast_to(
                code.astype(jnp.int32), (half, lanes)
            ).astype(jnp.int16)
            c = rs(i, way)
            c.start()
            sends.append(c)

    def cot_copy(k, receiving=False):
        slot = peers[k] if receiving else t
        return pltpu.make_async_remote_copy(
            src_ref=cot_v.at[slot] if receiving else cot_h.at[0],
            dst_ref=cot_v.at[slot],
            send_sem=cs.at[k],
            recv_sem=cr.at[k],
            **at("tensor", peers[k]),
        )

    def key_copy(k):
        return pltpu.make_async_remote_copy(
            src_ref=kp_v.at[peers[k]],
            dst_ref=kr_v.at[k],
            send_sem=ks.at[k],
            recv_sem=kr.at[k],
            **at("tensor", peers[k]),
        )

    def start_cot():
        for k in (1, 2, 0):
            c = cot_copy(k)
            c.start()
            sends.append(c)

    def slice_copy(i, receiving=False):
        to = lax.rem(r + i, R)
        slot = lax.rem(r + R - i, R) if receiving else r
        return pltpu.make_async_remote_copy(
            src_ref=ls_v.at[pl.ds(pl.multiple_of(to * orow, orow), orow)],
            dst_ref=ob_v.at[slot],
            send_sem=oas.at[i],
            recv_sem=oar.at[i],
            **at("replica", to),
        )

    def mean_copy(i, receiving=False):
        to = lax.rem(r + i, R)
        slot = lax.rem(r + R - i, R) if receiving else r
        cut = pl.ds(pl.multiple_of(slot * orow, orow), orow)
        return pltpu.make_async_remote_copy(
            src_ref=mean_v.at[cut],
            dst_ref=mean_v.at[cut],
            send_sem=obs.at[i],
            recv_sem=obr.at[i],
            **at("replica", to),
        )

    def outer_send():
        l_loc.wait()
        size = ls_v.shape[0]
        offset = offs_s[0]
        for f in range(1, offs_s.shape[0]):
            offset = jnp.where(frag_s[0] == f, offs_s[f], offset)
        picked = loc_v[:size, :].astype(F32)
        for b in range(1, loc_v.shape[0] // size):
            piece = loc_v[b * size:(b + 1) * size, :].astype(F32)
            picked = jnp.where(offset == b * size, piece, picked)
        ls_v[...] = picked.astype(jnp.bfloat16)
        for i in range(1, R):
            c = slice_copy(i)
            c.start()
            sends.append(c)

    def outer_mean():
        l_outer.wait()
        mine = pl.ds(pl.multiple_of(r * orow, orow), orow)
        base = outer_v[mine]
        total = base - ls_v[mine].astype(F32)
        for i in range(1, R):
            slice_copy(i, True).wait_recv()
            total = total + (base - ob_v[lax.rem(r + R - i, R)].astype(F32))
        mean_v[mine] = total / R
        for i in range(1, R):
            c = mean_copy(i)
            c.start()
            sends.append(c)

    outs = []

    def store(src, dst, i):
        c = pltpu.make_async_copy(src, dst, osem.at[i])
        c.start()
        outs.append(c)

    def outer_step():
        l_mom.wait()
        for i in range(1, R):
            mean_copy(i, True).wait_recv()
        mean = mean_v[...]
        moment = momentum_coef * mom_v[...] + mean
        mom_v[...] = moment
        sp_v[...] = outer_v[...] - outer_rate * (mean + momentum_coef * moment)
        store(mom_v, sm_o, 0)
        store(sp_v, sp_o, 1)

    def gradient():
        l_acts.wait()
        l_cot.wait()
        for k in range(len(peers)):
            cot_copy(k, True).wait_recv()
        cot = jnp.concatenate([cot_v[k] for k in range(T)], axis=1)
        piece = width // 4
        for c in range(4):
            cols = slice(c * piece, (c + 1) * piece)
            g_v[:, :, cols] = lax.dot_general(
                cot, acts_v[:, cols], (((0,), (0,)), ((), ())), preferred_element_type=F32
            ).reshape(n, rows, piece)

    def keys_part(far):
        u = (1 - side) if far else side
        block = w_v[pl.ds(u * 2 * per, 2 * per)].reshape(2 * per * rows, width)
        got = lax.dot_general(
            acts_v[...], block, (((1,), (1,)), ((), ())), preferred_element_type=F32
        )
        kp_v[2 * u] = got[:, :kt]
        kp_v[2 * u + 1] = got[:, kt:]
        for k in ((1, 2) if far else (0,)):
            c = key_copy(k)
            c.start()
            sends.append(c)

    def keys_end():
        for k in range(len(peers)):
            key_copy(k).wait_recv()
        k_v[...] = (((kp_v[t] + kr_v[0]) + kr_v[1]) + kr_v[2]).astype(jnp.bfloat16)
        store(k_v, keys_o.at[0], 2)

    start_cot()
    for tick in range(msgs + LAG):
        for k in range(max(CA, CR)):
            if tick < msgs and k < CA:
                ag_tick(tick * CA + k)
            if tick >= LAG and k < CR:
                rs_tick((tick - LAG) * CR + k)
        if tick == LAG - 1:
            gradient()
        if tick == min(LAG + 1, msgs - 1):
            outer_send()
        if tick == min(LAG + 4, msgs - 1):
            outer_mean()
        if tick == msgs - 1:
            l_w.wait()
            for m in range((msgs - 2) * CA, msgs * CA):
                for way in (0, 1):
                    ag(m, way, True).wait_recv()
            keys_part(True)
        if tick == msgs:
            keys_part(False)
            outer_step()
    keys_end()

    l_m1.wait()
    l_m2.wait()

    def finish(sub, col):
        iu = (msgs - 1 if sub == 0 else msgs - 2) * CR + col
        idn = (msgs - 2 if sub == 0 else msgs - 1) * CR + col
        rs(iu, 0).wait_recv()
        rs(idn, 1).wait_recv()
        su, sd = scale_of(ru_v, iu), scale_of(rd_v, idn)
        rr = slice(sub * half, (sub + 1) * half)
        for c in range(rtiles):
            here = slice(c * lanes, (c + 1) * lanes)
            cols = slice(col * rcut + c * lanes, col * rcut + (c + 1) * lanes)
            grad = (
                g_v[z, rr, cols]
                + ru_v[iu, :, here].astype(jnp.int32).astype(F32) * su
                + rd_v[idn, :, here].astype(jnp.int32).astype(F32) * sd
            )
            first = beta_first * m1_v[rr, cols] + (1.0 - beta_first) * grad
            second = beta_second * m2_v[rr, cols] + (1.0 - beta_second) * grad * grad
            w = w_v[z, rr, cols].astype(F32)
            new = w - adam_rate * (first / (jnp.sqrt(second) + adam_eps) + decay_coef * w)
            nw_v[rr, cols] = new.astype(jnp.bfloat16)
            m1_v[rr, cols] = first
            m2_v[rr, cols] = second

    for sub in (0, 1):
        for col in range(CR):
            finish(sub, col)
        cut = pl.ds(sub * half, half)
        store(m1_v.at[cut], nf_o.at[0, cut], 3 + 3 * sub)
        store(m2_v.at[cut], ns_o.at[0, cut], 4 + 3 * sub)
        store(nw_v.at[cut], nw_o.at[0, cut], 5 + 3 * sub)
    for c in sends:
        c.wait_send()
    for c in outs:
        c.wait()


def writer(*refs):
    k = len(refs) // 2
    sem = refs[-1]
    ins, outs = refs[:k], refs[k:2 * k]
    copies = [pltpu.make_async_copy(a, b, sem.at[i]) for i, (a, b) in enumerate(zip(ins, outs))]
    for c in copies:
        c.start()
    for c in copies:
        c.wait()


def solution(mesh):
    n, T, R = mesh.shape["fsdp"], mesh.shape["tensor"], mesh.shape["replica"]

    def on_device(acts, w, cot, m1, m2, loc, outer, mom, frag, offs):
        tok, width = acts.shape[1:]
        rows = w.shape[1]
        half = rows // 2
        kt = cot.shape[2]
        msgs = n - 1
        lanes = min(128, width)
        bf16 = jnp.bfloat16
        orow = outer.shape[0] // R
        any_ = pl.BlockSpec(memory_space=pl.ANY)
        smem = pl.BlockSpec(memory_space=pltpu.SMEM)
        ring = pltpu.VMEM((msgs * CR, half, width // CR + lanes), jnp.int16)
        dma = pltpu.SemaphoreType.DMA
        results = tuple(
            jax.ShapeDtypeStruct(*s)
            for s in (
                ((1, tok, kt), bf16),
                (w.shape, bf16),
                (m1.shape, F32),
                (m2.shape, F32),
                (outer.shape, F32),
                (mom.shape, F32),
            )
        )
        big_args = [
            pltpu.with_memory_space_constraint(a, pltpu.HBM)
            for a in (acts, w, cot, m1, m2, loc, outer, mom)
        ]
        held = pl.pallas_call(
            functools.partial(kernel, n, T, R),
            out_shape=results,
            in_specs=[pl.BlockSpec(memory_space=pltpu.HBM)] * 8 + [smem] * 2,
            out_specs=[any_] * 6,
            scratch_shapes=[
                pltpu.VMEM((tok, width), bf16),
                pltpu.VMEM((n, rows, width), bf16),
                pltpu.VMEM((T, tok, kt), bf16),
                pltpu.VMEM((n, rows, width), F32),
                pltpu.VMEM((rows, width), F32),
                pltpu.VMEM((rows, width), F32),
                pltpu.VMEM((rows, width), bf16),
                pltpu.VMEM((T, tok, kt), F32),
                pltpu.VMEM((T - 1, tok, kt), F32),
                pltpu.VMEM((tok, kt), bf16),
                pltpu.VMEM(loc.shape[1:], bf16),
                pltpu.VMEM(outer.shape, bf16),
                pltpu.VMEM(outer.shape, F32),
                pltpu.VMEM(outer.shape, F32),
                pltpu.VMEM((R, orow, outer.shape[1]), bf16),
                pltpu.VMEM(outer.shape, F32),
                pltpu.VMEM(outer.shape, F32),
                ring, ring, ring, ring,
                dma((8,)),
                dma((9,)),
                dma((2, msgs * CA)),
                dma((2, msgs * CA)),
                dma((2, msgs * CR)),
                dma((2, msgs * CR)),
                dma((T - 1,)),
                dma((T - 1,)),
                dma((T - 1,)),
                dma((T - 1,)),
                dma((R,)),
                dma((R,)),
                dma((R,)),
                dma((R,)),
            ],
            compiler_params=pltpu.CompilerParams(
                collective_id=0, has_side_effects=True, vmem_limit_bytes=40 * 2**20
            ),
        )(*big_args, frag, offs)
        return pl.pallas_call(
            writer,
            out_shape=results,
            in_specs=[any_] * 6,
            out_specs=[any_] * 6,
            scratch_shapes=[dma((6,))],
            compiler_params=pltpu.CompilerParams(vmem_limit_bytes=16 * 2**20),
        )(*[pltpu.with_memory_space_constraint(a, pltpu.VMEM) for a in held])

    big = P("replica", "fsdp", "tensor")
    flat = P(("fsdp", "tensor"), None)
    return jax.shard_map(
        on_device,
        mesh=mesh,
        in_specs=(big, big, big, big, big, P("replica", ("fsdp", "tensor"), None), flat, flat, P(), P()),
        out_specs=(big, big, big, big, flat, flat),
        check_vma=False,
    )
```

```python
import functools

import jax
import jax.numpy as jnp
from jax import lax
from jax.experimental import pallas as pl
from jax.experimental.pallas import tpu as pltpu
from jax.sharding import PartitionSpec as P

MESH = pl.DeviceIdType.MESH
F32 = jnp.float32
CA = 1
CR = 1
GRADIENT = 3
TOP = 32700.0
STEPS = 4.0

beta_first = 0.9
beta_second = 0.95
adam_rate = 0.001
adam_eps = 1e-08
decay_coef = 0.1
outer_rate = 0.7
momentum_coef = 0.9


def kernel(
    n, T, R,
    acts_h, w_h, cot_h, m1_h, m2_h, loc_h, outer_h, mom_h, frag_s, offs_h,
    keys_o, nw_o, nf_o, ns_o, sp_o, sm_o,
    acts_v, w_v, cot_v, g_v, m1_v, m2_v, nw_v, kp_v, kr_v, k_v,
    loc_v, ls_v, outer_v, mom_v, ob_v, mean_v, sp_v,
    su_v, sd_v, ru_v, rd_v, offs_s,
    lsem, osem, ags, agr, rss, rsr, cs, cr, ks, kr, oas, oar, obs, obr,
):
    z = lax.axis_index("fsdp")
    t = lax.axis_index("tensor")
    r = lax.axis_index("replica")
    h = n // 2
    up = lax.rem(z + 1, n)
    down = lax.rem(z + n - 1, n)
    rows = w_h.shape[1]
    half = rows // 2
    width = w_h.shape[2]
    lanes = min(128, width)
    kt = kp_v.shape[2]
    per = n // T
    orow = outer_h.shape[0] // R
    msgs = 2 * h - 1

    def at(axis, index):
        return dict(device_id={axis: index}, device_id_type=MESH)

    core = lax.rem(t, 2)
    side = t // 2
    sib = t + 1 - 2 * core
    peers = [sib, lax.rem(t + 2, 4), lax.rem(sib + 2, 4)]

    def load(src, dst, i):
        c = pltpu.make_async_copy(src, dst, lsem.at[i])
        c.start()
        return c

    barrier = pltpu.get_barrier_semaphore()
    for index in (up, down):
        pl.semaphore_signal(barrier, inc=1, **at("fsdp", index))
    for p in peers:
        pl.semaphore_signal(barrier, inc=1, **at("tensor", p))
    for i in range(1, R):
        pl.semaphore_signal(barrier, inc=1, **at("replica", lax.rem(r + i, R)))

    l_cot = load(cot_h.at[0], cot_v.at[t], 0)
    l_acts = load(acts_h.at[0], acts_v, 1)
    l_loc = load(loc_h.at[0], loc_v, 2)
    l_outer = load(outer_h, outer_v, 3)
    l_w = load(w_h.at[0], w_v.at[z], 4)
    l_mom = load(mom_h, mom_v, 5)
    l_m1 = load(m1_h.at[0], m1_v, 6)
    l_m2 = load(m2_h.at[0], m2_v, 7)
    l_offs = load(offs_h, offs_s, 8)

    pl.semaphore_wait(barrier, 2 + len(peers) + R - 1)

    acut = width // CA

    def ag(m, way, receiving=False):
        j, q = m // (2 * CA), m % (2 * CA)
        sub, col = (q // CA if way == 0 else 1 - q // CA), q % CA
        hop = j + (1 if receiving else 0)
        owner = lax.rem(z + n - hop, n) if way == 0 else lax.rem(z + hop, n)
        cut, cols = pl.ds(sub * half, half), pl.ds(col * acut, acut)
        own = j == 0 and not receiving
        src = w_h.at[0, cut, cols] if own else w_v.at[owner, cut, cols]
        return pltpu.make_async_remote_copy(
            src_ref=src,
            dst_ref=w_v.at[owner, cut, cols],
            send_sem=ags.at[way, m],
            recv_sem=agr.at[way, m],
            **at("fsdp", up if way == 0 else down),
        )

    sends = []

    def ag_tick(m):
        for way in (0, 1):
            if m >= 2 * CA:
                ag(m - 2 * CA, way, True).wait_recv()
            c = ag(m, way)
            c.start()
            sends.append(c)

    rcut = width // CR
    rtiles = rcut // lanes

    def rs_msg(i, way):
        main = 0 if way == 0 else 1
        if i < CR:
            return 0, main, i
        k = i - CR
        q = k % (2 * CR)
        return 1 + k // (2 * CR), (1 - main if q < CR else main), q % CR

    def rs(i, way):
        s_buf, r_buf = (su_v, ru_v) if way == 0 else (sd_v, rd_v)
        return pltpu.make_async_remote_copy(
            src_ref=s_buf.at[i],
            dst_ref=r_buf.at[i],
            send_sem=rss.at[way, i],
            recv_sem=rsr.at[way, i],
            **at("fsdp", up if way == 0 else down),
        )

    def scale_of(buf, i):
        code = buf[i, :, rcut:rcut + lanes].astype(jnp.int32).astype(F32)
        return jnp.exp2(code * (1.0 / STEPS)) * (1.0 / TOP)

    def rs_tick(i):
        for way in (0, 1):
            s, sub, col = rs_msg(i, way)
            s_buf, r_buf = (su_v, ru_v) if way == 0 else (sd_v, rd_v)
            d = lax.rem(z + n + h - s, n) if way == 0 else lax.rem(z + n - h + s, n)
            last = i - 2 * CR
            if last >= 0:
                rs(last, way).wait_recv()
                scale = scale_of(r_buf, last)
            sums, most = [], None
            for c in range(rtiles):
                here = slice(c * lanes, (c + 1) * lanes)
                whole = slice(col * rcut + c * lanes, col * rcut + (c + 1) * lanes)
                x = g_v[d, sub * half:(sub + 1) * half, whole]
                if last >= 0:
                    x = x + r_buf[last, :, here].astype(jnp.int32).astype(F32) * scale
                sums.append(x)
                a = jnp.abs(x)
                most = a if most is None else jnp.maximum(most, a)
            most = jnp.max(most, axis=0, keepdims=True)
            code = jnp.ceil(STEPS * jnp.log2(jnp.maximum(most, 1e-30)))
            inv = TOP * jnp.exp2(code * (-1.0 / STEPS))
            for c in range(rtiles):
                here = slice(c * lanes, (c + 1) * lanes)
                s_buf[i, :, here] = jnp.round(sums[c] * inv).astype(jnp.int32).astype(jnp.int16)
            s_buf[i, :, rcut:rcut + lanes] = jnp.broadcast_to(
                code.astype(jnp.int32), (half, lanes)
            ).astype(jnp.int16)
            c = rs(i, way)
            c.start()
            sends.append(c)

    def cot_copy(k, receiving=False):
        slot = peers[k] if receiving else t
        return pltpu.make_async_remote_copy(
            src_ref=cot_v.at[slot] if receiving else cot_h.at[0],
            dst_ref=cot_v.at[slot],
            send_sem=cs.at[k],
            recv_sem=cr.at[k],
            **at("tensor", peers[k]),
        )

    home = z // per
    turn = jnp.where(lax.rem(z, per) < per // 2, T - 1, 1)
    blocks = [home, lax.rem(home + turn, T), lax.rem(home + T - turn, T), lax.rem(home + T // 2, T)]

    def key_copy(o):
        b = blocks[o]
        slot = lax.rem(t - b + 2 * T - 1, T)
        return pltpu.make_async_remote_copy(
            src_ref=kp_v.at[b],
            dst_ref=kr_v.at[slot],
            send_sem=ks.at[o],
            recv_sem=kr.at[slot],
            **at("tensor", b),
        )

    def key_arrival(slot):
        return pltpu.make_async_remote_copy(
            src_ref=kp_v.at[0],
            dst_ref=kr_v.at[slot],
            send_sem=ks.at[0],
            recv_sem=kr.at[slot],
            **at("tensor", sib),
        )

    def start_cot():
        for k in (1, 2, 0):
            c = cot_copy(k)
            c.start()
            sends.append(c)

    def slice_copy(i, receiving=False):
        to = lax.rem(r + i, R)
        slot = lax.rem(r + R - i, R) if receiving else r
        return pltpu.make_async_remote_copy(
            src_ref=ls_v.at[pl.ds(pl.multiple_of(to * orow, orow), orow)],
            dst_ref=ob_v.at[slot],
            send_sem=oas.at[i],
            recv_sem=oar.at[i],
            **at("replica", to),
        )

    def mean_copy(i, receiving=False):
        to = lax.rem(r + i, R)
        slot = lax.rem(r + R - i, R) if receiving else r
        cut = pl.ds(pl.multiple_of(slot * orow, orow), orow)
        return pltpu.make_async_remote_copy(
            src_ref=mean_v.at[cut],
            dst_ref=mean_v.at[cut],
            send_sem=obs.at[i],
            recv_sem=obr.at[i],
            **at("replica", to),
        )

    def outer_send():
        l_loc.wait()
        l_offs.wait()
        size = ls_v.shape[0]
        offset = offs_s[0]
        for f in range(1, offs_s.shape[0]):
            offset = jnp.where(frag_s[0] == f, offs_s[f], offset)
        picked = loc_v[:size, :].astype(F32)
        for b in range(1, loc_v.shape[0] // size):
            piece = loc_v[b * size:(b + 1) * size, :].astype(F32)
            picked = jnp.where(offset == b * size, piece, picked)
        ls_v[...] = picked.astype(jnp.bfloat16)
        for i in range(1, R):
            c = slice_copy(i)
            c.start()
            sends.append(c)

    def outer_mean():
        l_outer.wait()
        mine = pl.ds(pl.multiple_of(r * orow, orow), orow)
        base = outer_v[mine]
        total = base - ls_v[mine].astype(F32)
        for i in range(1, R):
            slice_copy(i, True).wait_recv()
            total = total + (base - ob_v[lax.rem(r + R - i, R)].astype(F32))
        mean_v[mine] = total / R
        for i in range(1, R):
            c = mean_copy(i)
            c.start()
            sends.append(c)

    outs = []

    def store(src, dst, i):
        c = pltpu.make_async_copy(src, dst, osem.at[i])
        c.start()
        outs.append(c)

    def outer_step():
        l_mom.wait()
        for i in range(1, R):
            mean_copy(i, True).wait_recv()
        mean = mean_v[...]
        moment = momentum_coef * mom_v[...] + mean
        mom_v[...] = moment
        sp_v[...] = outer_v[...] - outer_rate * (mean + momentum_coef * moment)
        store(mom_v, sm_o, 0)
        store(sp_v, sp_o, 1)

    def gradient():
        l_acts.wait()
        l_cot.wait()
        for k in range(len(peers)):
            cot_copy(k, True).wait_recv()
        cot = jnp.concatenate([cot_v[k] for k in range(T)], axis=1)
        piece = width // 4
        for c in range(4):
            cols = slice(c * piece, (c + 1) * piece)
            g_v[:, :, cols] = lax.dot_general(
                cot, acts_v[:, cols], (((0,), (0,)), ((), ())), preferred_element_type=F32
            ).reshape(n, rows, piece)

    def key_block(o):
        b = blocks[o]
        block = w_v[pl.ds(b * per, per)].reshape(per * rows, width)
        kp_v[b] = lax.dot_general(
            acts_v[...], block, (((1,), (1,)), ((), ())), preferred_element_type=F32
        )

        @pl.when(t != b)
        def _():
            key_copy(o).start()

    def keys_end():
        for slot in range(T - 1):
            key_arrival(slot).wait_recv()
        k_v[...] = (((kp_v[t] + kr_v[0]) + kr_v[1]) + kr_v[2]).astype(jnp.bfloat16)
        store(k_v, keys_o.at[0], 2)

    def keys_sent():
        for o in range(T):
            @pl.when(t != blocks[o])
            def _():
                key_copy(o).wait_send()

    begin = min(GRADIENT, msgs - 1)
    late = msgs - 1
    first_keys = (7, 12) if msgs == 15 else (late, late)
    start_cot()
    l_w.wait()
    for tick in range(begin + msgs - 1):
        if tick < msgs:
            ag_tick(tick)
        if tick > begin:
            rs_tick(tick - begin + 1)
        if tick == begin:
            gradient()
            rs_tick(0)
            rs_tick(1)
        if tick == begin + 1:
            outer_send()
        if tick == begin + 4:
            outer_mean()
        if tick == late:
            for m in range(msgs - 2, msgs):
                for way in (0, 1):
                    ag(m, way, True).wait_recv()
        for o in (0, 1):
            if tick == first_keys[o]:
                key_block(o)
        if tick == late:
            key_block(2)
            key_block(3)
        if tick == begin + 7:
            outer_step()
    if begin + 4 >= begin + msgs - 1:
        outer_mean()
    if begin + 7 >= begin + msgs - 1:
        outer_step()
    keys_end()

    l_m1.wait()
    l_m2.wait()

    def finish(sub, col):
        iu = (msgs - 1 if sub == 0 else msgs - 2) * CR + col
        idn = (msgs - 2 if sub == 0 else msgs - 1) * CR + col
        rs(iu, 0).wait_recv()
        rs(idn, 1).wait_recv()
        su, sd = scale_of(ru_v, iu), scale_of(rd_v, idn)
        rr = slice(sub * half, (sub + 1) * half)
        for c in range(rtiles):
            here = slice(c * lanes, (c + 1) * lanes)
            cols = slice(col * rcut + c * lanes, col * rcut + (c + 1) * lanes)
            grad = (
                g_v[z, rr, cols]
                + ru_v[iu, :, here].astype(jnp.int32).astype(F32) * su
                + rd_v[idn, :, here].astype(jnp.int32).astype(F32) * sd
            )
            first = beta_first * m1_v[rr, cols] + (1.0 - beta_first) * grad
            second = beta_second * m2_v[rr, cols] + (1.0 - beta_second) * grad * grad
            w = w_v[z, rr, cols].astype(F32)
            new = w - adam_rate * (first / (jnp.sqrt(second) + adam_eps) + decay_coef * w)
            nw_v[rr, cols] = new.astype(jnp.bfloat16)
            m1_v[rr, cols] = first
            m2_v[rr, cols] = second

    for sub in (0, 1):
        for col in range(CR):
            finish(sub, col)
        cut = pl.ds(sub * half, half)
        store(m1_v.at[cut], nf_o.at[0, cut], 3 + 3 * sub)
        store(m2_v.at[cut], ns_o.at[0, cut], 4 + 3 * sub)
        store(nw_v.at[cut], nw_o.at[0, cut], 5 + 3 * sub)
    keys_sent()
    for c in sends:
        c.wait_send()
    for c in outs:
        c.wait()


def writer(*refs):
    k = len(refs) // 2
    sem = refs[-1]
    ins, outs = refs[:k], refs[k:2 * k]
    copies = [pltpu.make_async_copy(a, b, sem.at[i]) for i, (a, b) in enumerate(zip(ins, outs))]
    for c in copies:
        c.start()
    for c in copies:
        c.wait()


def solution(mesh):
    n, T, R = mesh.shape["fsdp"], mesh.shape["tensor"], mesh.shape["replica"]

    def on_device(acts, w, cot, m1, m2, loc, outer, mom, frag, offs):
        tok, width = acts.shape[1:]
        rows = w.shape[1]
        half = rows // 2
        kt = cot.shape[2]
        msgs = n - 1
        lanes = min(128, width)
        bf16 = jnp.bfloat16
        orow = outer.shape[0] // R
        hbm = pl.BlockSpec(memory_space=pltpu.HBM)
        any_ = pl.BlockSpec(memory_space=pl.ANY)
        ring = pltpu.VMEM((msgs * CR, half, width // CR + lanes), jnp.int16)
        dma = pltpu.SemaphoreType.DMA
        results = tuple(
            jax.ShapeDtypeStruct(*s)
            for s in (
                ((1, tok, kt), bf16),
                (w.shape, bf16),
                (m1.shape, F32),
                (m2.shape, F32),
                (outer.shape, F32),
                (mom.shape, F32),
            )
        )
        big_args = [
            pltpu.with_memory_space_constraint(a, pltpu.HBM)
            for a in (acts, w, cot, m1, m2, loc, outer, mom)
        ]
        held = pl.pallas_call(
            functools.partial(kernel, n, T, R),
            out_shape=results,
            in_specs=[hbm] * 8 + [pl.BlockSpec(memory_space=pltpu.SMEM), hbm],
            out_specs=[any_] * 6,
            scratch_shapes=[
                pltpu.VMEM((tok, width), bf16),
                pltpu.VMEM((n, rows, width), bf16),
                pltpu.VMEM((T, tok, kt), bf16),
                pltpu.VMEM((n, rows, width), F32),
                pltpu.VMEM((rows, width), F32),
                pltpu.VMEM((rows, width), F32),
                pltpu.VMEM((rows, width), bf16),
                pltpu.VMEM((T, tok, kt), F32),
                pltpu.VMEM((T, tok, kt), F32),
                pltpu.VMEM((tok, kt), bf16),
                pltpu.VMEM(loc.shape[1:], bf16),
                pltpu.VMEM(outer.shape, bf16),
                pltpu.VMEM(outer.shape, F32),
                pltpu.VMEM(outer.shape, F32),
                pltpu.VMEM((R, orow, outer.shape[1]), bf16),
                pltpu.VMEM(outer.shape, F32),
                pltpu.VMEM(outer.shape, F32),
                ring, ring, ring, ring,
                pltpu.SMEM(offs.shape, jnp.int32),
                dma((10,)),
                dma((9,)),
                dma((2, msgs * CA)),
                dma((2, msgs * CA)),
                dma((2, msgs * CR)),
                dma((2, msgs * CR)),
                dma((T - 1,)),
                dma((T - 1,)),
                dma((T,)),
                dma((T,)),
                dma((R,)),
                dma((R,)),
                dma((R,)),
                dma((R,)),
            ],
            compiler_params=pltpu.CompilerParams(
                collective_id=0, has_side_effects=True, vmem_limit_bytes=40 * 2**20
            ),
        )(*big_args, frag, pltpu.with_memory_space_constraint(offs, pltpu.HBM))
        return pl.pallas_call(
            writer,
            out_shape=results,
            in_specs=[any_] * 6,
            out_specs=[any_] * 6,
            scratch_shapes=[dma((6,))],
            compiler_params=pltpu.CompilerParams(vmem_limit_bytes=16 * 2**20),
        )(*[pltpu.with_memory_space_constraint(a, pltpu.VMEM) for a in held])

    big = P("replica", "fsdp", "tensor")
    flat = P(("fsdp", "tensor"), None)
    return jax.shard_map(
        on_device,
        mesh=mesh,
        in_specs=(big, big, big, big, big, P("replica", ("fsdp", "tensor"), None), flat, flat, P(), P()),
        out_specs=(big, big, big, big, flat, flat),
        check_vma=False,
    )
```

```python
import functools

import jax
import jax.numpy as jnp
from jax import lax
from jax.experimental import pallas as pl
from jax.experimental.pallas import tpu as pltpu
from jax.sharding import PartitionSpec as P

MESH = pl.DeviceIdType.MESH
F32 = jnp.float32
CA = 1
CR = 1
GRADIENT = 3
TOP = 32700.0
STEPS = 4.0

beta_first = 0.9
beta_second = 0.95
adam_rate = 0.001
adam_eps = 1e-08
decay_coef = 0.1
outer_rate = 0.7
momentum_coef = 0.9


def kernel(
    n, T, R,
    acts_h, w_h, cot_h, m1_h, m2_h, loc_h, outer_h, mom_h, frag_s, offs_h,
    keys_o, nw_o, nf_o, ns_o, sp_o, sm_o,
    acts_v, w_v, cot_v, g_v, m1_v, m2_v, nw_v, kp_v, kr_v, k_v,
    loc_v, ls_v, outer_v, mom_v, ob_v, mean_v, sp_v,
    su_v, sd_v, ru_v, rd_v, offs_s,
    lsem, osem, ags, agr, rss, rsr, cs, cr, ks, kr, oas, oar, obs, obr,
):
    z = lax.axis_index("fsdp")
    t = lax.axis_index("tensor")
    r = lax.axis_index("replica")
    h = n // 2
    up = lax.rem(z + 1, n)
    down = lax.rem(z + n - 1, n)
    rows = w_h.shape[1]
    half = rows // 2
    width = w_h.shape[2]
    lanes = min(128, width)
    kt = kp_v.shape[2]
    per = n // T
    orow = outer_h.shape[0] // R
    msgs = 2 * h - 1

    def at(axis, index):
        return dict(device_id={axis: index}, device_id_type=MESH)

    core = lax.rem(t, 2)
    side = t // 2
    sib = t + 1 - 2 * core
    peers = [sib, lax.rem(t + 2, 4), lax.rem(sib + 2, 4)]

    def load(src, dst, i):
        c = pltpu.make_async_copy(src, dst, lsem.at[i])
        c.start()
        return c

    barrier = pltpu.get_barrier_semaphore()
    for index in (up, down):
        pl.semaphore_signal(barrier, inc=1, **at("fsdp", index))
    for p in peers:
        pl.semaphore_signal(barrier, inc=1, **at("tensor", p))
    for i in range(1, R):
        pl.semaphore_signal(barrier, inc=1, **at("replica", lax.rem(r + i, R)))

    l_cot = load(cot_h.at[0], cot_v.at[t], 0)
    l_acts = load(acts_h.at[0], acts_v, 1)
    l_loc = load(loc_h.at[0], loc_v, 2)
    l_outer = load(outer_h, outer_v, 3)
    l_w = load(w_h.at[0], w_v.at[z], 4)
    l_mom = load(mom_h, mom_v, 5)
    l_m1 = load(m1_h.at[0], m1_v, 6)
    l_m2 = load(m2_h.at[0], m2_v, 7)
    l_offs = load(offs_h, offs_s, 8)

    pl.semaphore_wait(barrier, 2 + len(peers) + R - 1)

    acut = width // CA

    def ag(m, way, receiving=False):
        j, q = m // (2 * CA), m % (2 * CA)
        sub, col = (q // CA if way == 0 else 1 - q // CA), q % CA
        hop = j + (1 if receiving else 0)
        owner = lax.rem(z + n - hop, n) if way == 0 else lax.rem(z + hop, n)
        cut, cols = pl.ds(sub * half, half), pl.ds(col * acut, acut)
        own = j == 0 and not receiving
        src = w_h.at[0, cut, cols] if own else w_v.at[owner, cut, cols]
        return pltpu.make_async_remote_copy(
            src_ref=src,
            dst_ref=w_v.at[owner, cut, cols],
            send_sem=ags.at[way, m],
            recv_sem=agr.at[way, m],
            **at("fsdp", up if way == 0 else down),
        )

    sends = []

    def ag_tick(m):
        for way in (0, 1):
            if m >= 2 * CA:
                ag(m - 2 * CA, way, True).wait_recv()
            c = ag(m, way)
            c.start()
            sends.append(c)

    rcut = width // CR
    rtiles = rcut // lanes

    def rs_msg(i, way):
        main = 0 if way == 0 else 1
        if i < CR:
            return 0, main, i
        k = i - CR
        q = k % (2 * CR)
        return 1 + k // (2 * CR), (1 - main if q < CR else main), q % CR

    def rs(i, way):
        s_buf, r_buf = (su_v, ru_v) if way == 0 else (sd_v, rd_v)
        return pltpu.make_async_remote_copy(
            src_ref=s_buf.at[i],
            dst_ref=r_buf.at[i],
            send_sem=rss.at[way, i],
            recv_sem=rsr.at[way, i],
            **at("fsdp", up if way == 0 else down),
        )

    def scale_of(buf, i):
        code = buf[i, :, rcut:rcut + lanes].astype(jnp.int32).astype(F32)
        return jnp.exp2(code * (1.0 / STEPS)) * (1.0 / TOP)

    def rs_tick(i):
        for way in (0, 1):
            s, sub, col = rs_msg(i, way)
            s_buf, r_buf = (su_v, ru_v) if way == 0 else (sd_v, rd_v)
            d = lax.rem(z + n + h - s, n) if way == 0 else lax.rem(z + n - h + s, n)
            last = i - 2 * CR
            if last >= 0:
                rs(last, way).wait_recv()
                scale = scale_of(r_buf, last)
            sums, most = [], None
            for c in range(rtiles):
                here = slice(c * lanes, (c + 1) * lanes)
                whole = slice(col * rcut + c * lanes, col * rcut + (c + 1) * lanes)
                x = g_v[d, sub * half:(sub + 1) * half, whole]
                if last >= 0:
                    x = x + r_buf[last, :, here].astype(jnp.int32).astype(F32) * scale
                sums.append(x)
                a = jnp.abs(x)
                most = a if most is None else jnp.maximum(most, a)
            most = jnp.max(most, axis=0, keepdims=True)
            code = jnp.ceil(STEPS * jnp.log2(jnp.maximum(most, 1e-30)))
            inv = TOP * jnp.exp2(code * (-1.0 / STEPS))
            for c in range(rtiles):
                here = slice(c * lanes, (c + 1) * lanes)
                s_buf[i, :, here] = jnp.round(sums[c] * inv).astype(jnp.int32).astype(jnp.int16)
            s_buf[i, :, rcut:rcut + lanes] = jnp.broadcast_to(
                code.astype(jnp.int32), (half, lanes)
            ).astype(jnp.int16)
            c = rs(i, way)
            c.start()
            sends.append(c)

    def cot_copy(k, receiving=False):
        slot = peers[k] if receiving else t
        return pltpu.make_async_remote_copy(
            src_ref=cot_v.at[slot] if receiving else cot_h.at[0],
            dst_ref=cot_v.at[slot],
            send_sem=cs.at[k],
            recv_sem=cr.at[k],
            **at("tensor", peers[k]),
        )

    home = z // per
    turn = jnp.where(lax.rem(z, per) < per // 2, T - 1, 1)
    blocks = [home, lax.rem(home + turn, T), lax.rem(home + T - turn, T), lax.rem(home + T // 2, T)]

    def key_copy(o):
        b = blocks[o]
        slot = lax.rem(t - b + 2 * T - 1, T)
        return pltpu.make_async_remote_copy(
            src_ref=kp_v.at[b],
            dst_ref=kr_v.at[slot],
            send_sem=ks.at[o],
            recv_sem=kr.at[slot],
            **at("tensor", b),
        )

    def key_arrival(slot):
        return pltpu.make_async_remote_copy(
            src_ref=kp_v.at[0],
            dst_ref=kr_v.at[slot],
            send_sem=ks.at[0],
            recv_sem=kr.at[slot],
            **at("tensor", sib),
        )

    def start_cot():
        for k in (1, 2, 0):
            c = cot_copy(k)
            c.start()
            sends.append(c)

    def slice_copy(i, receiving=False):
        to = lax.rem(r + i, R)
        slot = lax.rem(r + R - i, R) if receiving else r
        return pltpu.make_async_remote_copy(
            src_ref=ls_v.at[pl.ds(pl.multiple_of(to * orow, orow), orow)],
            dst_ref=ob_v.at[slot],
            send_sem=oas.at[i],
            recv_sem=oar.at[i],
            **at("replica", to),
        )

    def mean_copy(i, receiving=False):
        to = lax.rem(r + i, R)
        slot = lax.rem(r + R - i, R) if receiving else r
        cut = pl.ds(pl.multiple_of(slot * orow, orow), orow)
        return pltpu.make_async_remote_copy(
            src_ref=mean_v.at[cut],
            dst_ref=mean_v.at[cut],
            send_sem=obs.at[i],
            recv_sem=obr.at[i],
            **at("replica", to),
        )

    def outer_send():
        l_loc.wait()
        l_offs.wait()
        size = ls_v.shape[0]
        offset = offs_s[0]
        for f in range(1, offs_s.shape[0]):
            offset = jnp.where(frag_s[0] == f, offs_s[f], offset)
        picked = loc_v[:size, :].astype(F32)
        for b in range(1, loc_v.shape[0] // size):
            piece = loc_v[b * size:(b + 1) * size, :].astype(F32)
            picked = jnp.where(offset == b * size, piece, picked)
        ls_v[...] = picked.astype(jnp.bfloat16)
        for i in range(1, R):
            c = slice_copy(i)
            c.start()
            sends.append(c)

    def outer_mean():
        l_outer.wait()
        mine = pl.ds(pl.multiple_of(r * orow, orow), orow)
        base = outer_v[mine]
        total = base - ls_v[mine].astype(F32)
        for i in range(1, R):
            slice_copy(i, True).wait_recv()
            total = total + (base - ob_v[lax.rem(r + R - i, R)].astype(F32))
        mean_v[mine] = total / R
        for i in range(1, R):
            c = mean_copy(i)
            c.start()
            sends.append(c)

    outs = []

    def store(src, dst, i):
        c = pltpu.make_async_copy(src, dst, osem.at[i])
        c.start()
        outs.append(c)

    def outer_step():
        l_mom.wait()
        for i in range(1, R):
            mean_copy(i, True).wait_recv()
        mean = mean_v[...]
        moment = momentum_coef * mom_v[...] + mean
        mom_v[...] = moment
        sp_v[...] = outer_v[...] - outer_rate * (mean + momentum_coef * moment)
        store(mom_v, sm_o, 0)
        store(sp_v, sp_o, 1)

    def gradient():
        l_acts.wait()
        l_cot.wait()
        for k in range(len(peers)):
            cot_copy(k, True).wait_recv()
        cot = jnp.concatenate([cot_v[k] for k in range(T)], axis=1)
        piece = width // 4
        for c in range(4):
            cols = slice(c * piece, (c + 1) * piece)
            g_v[:, :, cols] = lax.dot_general(
                cot, acts_v[:, cols], (((0,), (0,)), ((), ())), preferred_element_type=F32
            ).reshape(n, rows, piece)

    def key_block(o):
        b = blocks[o]
        block = w_v[pl.ds(b * per, per)].reshape(per * rows, width)
        kp_v[b] = lax.dot_general(
            acts_v[...], block, (((1,), (1,)), ((), ())), preferred_element_type=F32
        )

        @pl.when(t != b)
        def _():
            key_copy(o).start()

    def keys_end():
        for slot in range(T - 1):
            key_arrival(slot).wait_recv()
        k_v[...] = (((kp_v[t] + kr_v[0]) + kr_v[1]) + kr_v[2]).astype(jnp.bfloat16)
        store(k_v, keys_o.at[0], 2)

    def keys_sent():
        for o in range(T):
            @pl.when(t != blocks[o])
            def _():
                key_copy(o).wait_send()

    begin = min(GRADIENT, msgs - 1)
    late = msgs - 1
    first_keys = (7, 12) if msgs == 15 else (late, late)
    for tick in range(begin + msgs - 1):
        if tick < msgs:
            ag_tick(tick)
        if tick == 0:
            start_cot()
        if tick > begin:
            rs_tick(tick - begin + 1)
        if tick == begin:
            gradient()
            rs_tick(0)
            rs_tick(1)
        if tick == min(1, late):
            outer_send()
        if tick == begin + 4:
            outer_mean()
        if tick == late:
            for m in range(msgs - 2, msgs):
                for way in (0, 1):
                    ag(m, way, True).wait_recv()
        if tick == first_keys[0]:
            l_w.wait()
        for o in (0, 1):
            if tick == first_keys[o]:
                key_block(o)
        if tick == late:
            key_block(2)
        if tick == late + 1:
            key_block(3)
        if tick == begin + 7:
            outer_step()
    if begin + 4 >= begin + msgs - 1:
        outer_mean()
    if begin + 7 >= begin + msgs - 1:
        outer_step()
    l_m1.wait()
    l_m2.wait()

    def finish(sub, col):
        iu = (msgs - 1 if sub == 0 else msgs - 2) * CR + col
        idn = (msgs - 2 if sub == 0 else msgs - 1) * CR + col
        rs(iu, 0).wait_recv()
        rs(idn, 1).wait_recv()
        su, sd = scale_of(ru_v, iu), scale_of(rd_v, idn)
        rr = slice(sub * half, (sub + 1) * half)
        for c in range(rtiles):
            here = slice(c * lanes, (c + 1) * lanes)
            cols = slice(col * rcut + c * lanes, col * rcut + (c + 1) * lanes)
            grad = (
                g_v[z, rr, cols]
                + ru_v[iu, :, here].astype(jnp.int32).astype(F32) * su
                + rd_v[idn, :, here].astype(jnp.int32).astype(F32) * sd
            )
            first = beta_first * m1_v[rr, cols] + (1.0 - beta_first) * grad
            second = beta_second * m2_v[rr, cols] + (1.0 - beta_second) * grad * grad
            w = w_v[z, rr, cols].astype(F32)
            new = w - adam_rate * (first / (jnp.sqrt(second) + adam_eps) + decay_coef * w)
            nw_v[rr, cols] = new.astype(jnp.bfloat16)
            m1_v[rr, cols] = first
            m2_v[rr, cols] = second

    for sub in (0, 1):
        for col in range(CR):
            finish(sub, col)
        cut = pl.ds(sub * half, half)
        store(m1_v.at[cut], nf_o.at[0, cut], 3 + 3 * sub)
        store(m2_v.at[cut], ns_o.at[0, cut], 4 + 3 * sub)
        store(nw_v.at[cut], nw_o.at[0, cut], 5 + 3 * sub)
    keys_end()
    keys_sent()
    for c in sends:
        c.wait_send()
    for c in outs:
        c.wait()


def writer(*refs):
    k = len(refs) // 2
    sem = refs[-1]
    ins, outs = refs[:k], refs[k:2 * k]
    copies = [pltpu.make_async_copy(a, b, sem.at[i]) for i, (a, b) in enumerate(zip(ins, outs))]
    for c in copies:
        c.start()
    for c in copies:
        c.wait()


def solution(mesh):
    n, T, R = mesh.shape["fsdp"], mesh.shape["tensor"], mesh.shape["replica"]

    def on_device(acts, w, cot, m1, m2, loc, outer, mom, frag, offs):
        tok, width = acts.shape[1:]
        rows = w.shape[1]
        half = rows // 2
        kt = cot.shape[2]
        msgs = n - 1
        lanes = min(128, width)
        bf16 = jnp.bfloat16
        orow = outer.shape[0] // R
        hbm = pl.BlockSpec(memory_space=pltpu.HBM)
        any_ = pl.BlockSpec(memory_space=pl.ANY)
        ring = pltpu.VMEM((msgs * CR, half, width // CR + lanes), jnp.int16)
        dma = pltpu.SemaphoreType.DMA
        results = tuple(
            jax.ShapeDtypeStruct(*s)
            for s in (
                ((1, tok, kt), bf16),
                (w.shape, bf16),
                (m1.shape, F32),
                (m2.shape, F32),
                (outer.shape, F32),
                (mom.shape, F32),
            )
        )
        big_args = [
            pltpu.with_memory_space_constraint(a, pltpu.HBM)
            for a in (acts, w, cot, m1, m2, loc, outer, mom)
        ]
        held = pl.pallas_call(
            functools.partial(kernel, n, T, R),
            out_shape=results,
            in_specs=[hbm] * 8 + [pl.BlockSpec(memory_space=pltpu.SMEM), hbm],
            out_specs=[any_] * 6,
            scratch_shapes=[
                pltpu.VMEM((tok, width), bf16),
                pltpu.VMEM((n, rows, width), bf16),
                pltpu.VMEM((T, tok, kt), bf16),
                pltpu.VMEM((n, rows, width), F32),
                pltpu.VMEM((rows, width), F32),
                pltpu.VMEM((rows, width), F32),
                pltpu.VMEM((rows, width), bf16),
                pltpu.VMEM((T, tok, kt), F32),
                pltpu.VMEM((T, tok, kt), F32),
                pltpu.VMEM((tok, kt), bf16),
                pltpu.VMEM(loc.shape[1:], bf16),
                pltpu.VMEM(outer.shape, bf16),
                pltpu.VMEM(outer.shape, F32),
                pltpu.VMEM(outer.shape, F32),
                pltpu.VMEM((R, orow, outer.shape[1]), bf16),
                pltpu.VMEM(outer.shape, F32),
                pltpu.VMEM(outer.shape, F32),
                ring, ring, ring, ring,
                pltpu.SMEM(offs.shape, jnp.int32),
                dma((10,)),
                dma((9,)),
                dma((2, msgs * CA)),
                dma((2, msgs * CA)),
                dma((2, msgs * CR)),
                dma((2, msgs * CR)),
                dma((T - 1,)),
                dma((T - 1,)),
                dma((T,)),
                dma((T,)),
                dma((R,)),
                dma((R,)),
                dma((R,)),
                dma((R,)),
            ],
            compiler_params=pltpu.CompilerParams(
                collective_id=0, has_side_effects=True, vmem_limit_bytes=40 * 2**20
            ),
        )(*big_args, frag, pltpu.with_memory_space_constraint(offs, pltpu.HBM))
        return pl.pallas_call(
            writer,
            out_shape=results,
            in_specs=[any_] * 6,
            out_specs=[any_] * 6,
            scratch_shapes=[dma((6,))],
            compiler_params=pltpu.CompilerParams(vmem_limit_bytes=16 * 2**20),
        )(*[pltpu.with_memory_space_constraint(a, pltpu.VMEM) for a in held])

    big = P("replica", "fsdp", "tensor")
    flat = P(("fsdp", "tensor"), None)
    return jax.shard_map(
        on_device,
        mesh=mesh,
        in_specs=(big, big, big, big, big, P("replica", ("fsdp", "tensor"), None), flat, flat, P(), P()),
        out_specs=(big, big, big, big, flat, flat),
        check_vma=False,
    )
```
